128 devices in a mesh: dp: 8 (over x, core), ctx: 16 (over y, z).
Axes of the slice: x: 4, y: 4, z: 4, core: 2. Of those that a mesh axis runs over, the one named last changes fastest.
Arguments:
- query_matrix: bfloat16 [16384, 4096], P(('dp', 'ctx')), may hold values from -162 to 162
- key_matrix: bfloat16 [16384, 512], P(('dp', 'ctx')), may hold values from -6 to 6
- value_matrix: bfloat16 [16384, 512], P(('dp', 'ctx')), may hold values from -6 to 6
- output_gradient: bfloat16 [16384, 4096], P(('dp', 'ctx')), may hold values from -6 to 6
- document_length_list: int32 [96], replicated, may hold values from 1 to 256, 16384 in all
- slab_plan: int32 [8, 16, 16], P('dp'), may hold values from 0 to 15, as said below
Outputs:
- attended: bfloat16 [16384, 4096], P(('dp', 'ctx'))
- query_grads: bfloat16 [16384, 4096], P(('dp', 'ctx'))
- key_grads: bfloat16 [16384, 512], P(('dp', 'ctx'))
- value_grads: bfloat16 [16384, 512], P(('dp', 'ctx'))
The draws below stay inside these ranges and needn't reach their ends.
Inputs may be any that keep to these rules, and one draw needn't show every extreme that they name: `document_length_list`: the lengths add up to 16384 and the longest is exactly 256. For every g and o, slab_plan[g, o, :] names each of 0 to 15 once.
All inputs are finite; a program needn't handle non-finite values.
Results may differ from the reference program's by a relative error of at most 0.04.
Values may be sent and summed in bfloat16 or wider, within the bound.
A program may use at most 128 MiB of HBM per device.

```python
import math
import jax
import jax.numpy as jnp
import numpy as np
from jax import lax

QUERY_HEADS = 32
KEY_VALUE_HEADS = 4
HEAD_WIDTH = 128
TOK_DEV = 128
PACKED_TOKENS = 16384
LONGEST_LENGTH = 256
DOCS = 96
GROUPS = 8
SPLIT = 16


def key_base(key):
    return jax.random.truncated_normal(jax.random.fold_in(key, 11), -6.0, 6.0, (PACKED_TOKENS, KEY_VALUE_HEADS * HEAD_WIDTH), jnp.float32)


def permuted_row(sub_key):
    return jax.random.permutation(sub_key, SPLIT)


def draw_key_matrix(key, part):
    starting_keys = key_base(key)
    return starting_keys.astype(jnp.bfloat16)


def draw_query_matrix(key, part):
    key = jax.random.fold_in(key, 4)
    queries = jax.random.truncated_normal(key, -6.0, 6.0, (PACKED_TOKENS, QUERY_HEADS * HEAD_WIDTH), jnp.float32)
    return queries.astype(jnp.bfloat16)


def draw_slab_plan(key, part):
    key = jax.random.fold_in(key, 5)
    many_keys = jax.random.split(key, GROUPS * SPLIT)
    rows_all = jax.vmap(permuted_row)(many_keys)
    return rows_all.reshape(GROUPS, SPLIT, SPLIT).astype(jnp.int32)


def levels(own_key, extent, shards, smallest, largest):
    def one(position, shards_of):
        heights = jax.random.uniform(jax.random.fold_in(jax.random.fold_in(own_key, 6), position), (shards_of,), jnp.float32, smallest / len(shards), largest / len(shards))
        return jnp.repeat(jnp.exp(heights), extent[position] // shards_of).reshape((-1,) + (1,) * (len(extent) - position - 1))

    gain = one(*shards[0])
    for cut in shards[1:]:
        gain = gain * one(*cut)
    return gain


def profile(number_of, total, most, lean):
    loads = [(1 << 20) // math.isqrt(standing ** lean) + 1 for standing in range(2, number_of + 1)]
    spare, given = total - most - (number_of - 1), [1] * (number_of - 1)
    while spare > 0:
        movable = [i for i in range(number_of - 1) if given[i] < most]
        whole, budget = sum([loads[i] for i in movable]), spare
        for i in movable:
            more = min(most - given[i], max(1, budget * loads[i] // whole), spare)
            given[i] = given[i] + more
            spare = spare - more
    return np.array([most] + given)


def uneven_parts(rng, number_of, total, bound, slope):
    if number_of == 2:
        one = jax.random.randint(rng, (), max(1, total - bound), min(bound, total - 1) + 1)
        return jnp.stack([one, total - one])
    tallies = jnp.asarray(profile(number_of, total, bound, slope), jnp.int32)
    twos = (number_of - 1) // 2
    giver, taker = tallies[1:1 + 2 * twos:2], tallies[2:2 + 2 * twos:2]
    room = jnp.minimum(giver - 1, bound - taker)
    shifted = jax.random.randint(jax.random.fold_in(rng, 1), (twos,), 0, 1 << 20) % (room + 1)
    tallies = tallies.at[1:1 + 2 * twos:2].set(giver - shifted).at[2:2 + 2 * twos:2].set(taker + shifted)
    return tallies[jax.random.permutation(jax.random.fold_in(rng, 2), number_of)]


def gaussian(own_key, dims, scale, limit, cuts=(), kind=jnp.bfloat16):
    gain = levels(own_key, dims, cuts, -0.22, 0.18) if cuts else 1.0
    entries = jax.random.normal(own_key, dims, jnp.float32) * scale * gain
    return jnp.minimum(jnp.maximum(entries, -limit), limit).astype(kind)


def setup_inputs(seed: int = 0) -> dict:
    seeds = jax.random.split(jax.random.key(seed), 7)
    query_matrix = draw_query_matrix(jax.random.fold_in(seeds[6], 71), 0)
    key_matrix = draw_key_matrix(jax.random.fold_in(seeds[6], 71), 0)
    value_matrix = gaussian(seeds[2], (PACKED_TOKENS, KEY_VALUE_HEADS * HEAD_WIDTH), 1.0, 6.0, ((0, 128),))
    output_gradient = gaussian(seeds[3], (PACKED_TOKENS, QUERY_HEADS * HEAD_WIDTH), 1.0, 6.0, ((0, 128),))
    document_length_list = uneven_parts(seeds[4], DOCS, PACKED_TOKENS, LONGEST_LENGTH, 2).astype(jnp.int32)
    slab_plan = draw_slab_plan(jax.random.fold_in(seeds[6], 71), 0)
    return dict(query_matrix=query_matrix, key_matrix=key_matrix, value_matrix=value_matrix, output_gradient=output_gradient, document_length_list=document_length_list, slab_plan=slab_plan)


def doc_first(positions, document_length_list):
    doc_ends = jnp.cumsum(document_length_list).astype(jnp.int32)
    ended = doc_ends[None, :] <= positions[:, None]
    return lax.optimization_barrier(jnp.sum(jnp.where(ended, document_length_list[None, :], 0), axis=1)).astype(jnp.int32)

def reference(query_matrix, key_matrix, value_matrix, output_gradient, document_length_list, slab_plan):
    heads_per_group = QUERY_HEADS // KEY_VALUE_HEADS
    scale = 1.0 / math.sqrt(HEAD_WIDTH)
    rows_per_block = min(128, PACKED_TOKENS)
    visible_span = LONGEST_LENGTH + rows_per_block
    padded_keys = jnp.concatenate([jnp.zeros((LONGEST_LENGTH, KEY_VALUE_HEADS * HEAD_WIDTH), key_matrix.dtype), key_matrix], axis=0)
    padded_values = jnp.concatenate([jnp.zeros((LONGEST_LENGTH, KEY_VALUE_HEADS * HEAD_WIDTH), value_matrix.dtype), value_matrix], axis=0)
    empty_accumulator = jnp.zeros((PACKED_TOKENS + LONGEST_LENGTH, KEY_VALUE_HEADS * HEAD_WIDTH), jnp.float32)

    def step(carry, block_idx):
        key_accumulator, value_accumulator = carry
        first_row_offset = (block_idx * rows_per_block).astype(jnp.int32)
        query_block_tile = lax.dynamic_slice(query_matrix, (first_row_offset, jnp.int32(0)), (rows_per_block, QUERY_HEADS * HEAD_WIDTH)).astype(jnp.float32).reshape(rows_per_block, KEY_VALUE_HEADS, heads_per_group, HEAD_WIDTH)
        delta_block = lax.dynamic_slice(output_gradient, (first_row_offset, jnp.int32(0)), (rows_per_block, QUERY_HEADS * HEAD_WIDTH)).astype(jnp.float32).reshape(rows_per_block, KEY_VALUE_HEADS, heads_per_group, HEAD_WIDTH)
        key_block_tile = lax.dynamic_slice(padded_keys, (first_row_offset, jnp.int32(0)), (visible_span, KEY_VALUE_HEADS * HEAD_WIDTH)).astype(jnp.float32).reshape(visible_span, KEY_VALUE_HEADS, HEAD_WIDTH)
        value_block_tile = lax.dynamic_slice(padded_values, (first_row_offset, jnp.int32(0)), (visible_span, KEY_VALUE_HEADS * HEAD_WIDTH)).astype(jnp.float32).reshape(visible_span, KEY_VALUE_HEADS, HEAD_WIDTH)
        q_pos = (first_row_offset + jnp.arange(rows_per_block, dtype=jnp.int32)).astype(jnp.int32)
        k_pos = (first_row_offset - LONGEST_LENGTH + jnp.arange(visible_span, dtype=jnp.int32)).astype(jnp.int32)
        first_pos = doc_first(q_pos, document_length_list)
        visible = (k_pos[None, :] >= first_pos[:, None]) & (k_pos[None, :] <= q_pos[:, None])
        scores = jnp.einsum('ikgd,jkd->kgij', query_block_tile, key_block_tile) * scale
        scores = jnp.where(visible[None, None], scores, jnp.float32(-1e+30))
        row_max = lax.optimization_barrier(jnp.max(scores, axis=-1, keepdims=True))
        log_sum = row_max + jnp.log(lax.optimization_barrier(jnp.sum(jnp.exp(scores - row_max), axis=-1, keepdims=True)))
        probs = jnp.exp(scores - log_sum)
        probability_block = lax.optimization_barrier(probs.astype(jnp.bfloat16)).astype(jnp.float32)
        out_b = lax.optimization_barrier(jnp.einsum('kgij,jkd->ikgd', probability_block, value_block_tile).astype(jnp.bfloat16))
        out_f = out_b.astype(jnp.float32)
        delta = jnp.transpose(lax.optimization_barrier(jnp.sum(delta_block * out_f, axis=-1)), (1, 2, 0))
        d_probs = jnp.einsum('ikgd,jkd->kgij', delta_block, value_block_tile)
        scores_gradient = lax.optimization_barrier((probs * (d_probs - delta[..., None]) * scale).astype(jnp.bfloat16)).astype(jnp.float32)
        dq_b = jnp.einsum('kgij,jkd->ikgd', scores_gradient, key_block_tile).astype(jnp.bfloat16)
        key_gradient_share = jnp.einsum('ptlv,lptr->vpr', scores_gradient, query_block_tile).reshape(visible_span, KEY_VALUE_HEADS * HEAD_WIDTH)
        value_gradient_share = jnp.einsum('ptlv,lptr->vpr', probability_block, delta_block).reshape(visible_span, KEY_VALUE_HEADS * HEAD_WIDTH)
        key_accumulator = lax.dynamic_update_slice(key_accumulator, lax.dynamic_slice(key_accumulator, (first_row_offset, jnp.int32(0)), (visible_span, KEY_VALUE_HEADS * HEAD_WIDTH)) + key_gradient_share, (first_row_offset, jnp.int32(0)))
        value_accumulator = lax.dynamic_update_slice(value_accumulator, lax.dynamic_slice(value_accumulator, (first_row_offset, jnp.int32(0)), (visible_span, KEY_VALUE_HEADS * HEAD_WIDTH)) + value_gradient_share, (first_row_offset, jnp.int32(0)))
        return ((key_accumulator, value_accumulator), (out_b.reshape(rows_per_block, QUERY_HEADS * HEAD_WIDTH), dq_b.reshape(rows_per_block, QUERY_HEADS * HEAD_WIDTH)))
    (key_accumulator, value_accumulator), (out_blocks, dq_blocks) = lax.scan(step, (empty_accumulator, empty_accumulator), jnp.arange(PACKED_TOKENS // rows_per_block, dtype=jnp.int32))
    out_nat = out_blocks.reshape(PACKED_TOKENS, QUERY_HEADS * HEAD_WIDTH)
    dq_nat = dq_blocks.reshape(PACKED_TOKENS, QUERY_HEADS * HEAD_WIDTH)
    slab_rows = TOK_DEV // SPLIT
    group_ids = jnp.arange(GROUPS, dtype=jnp.int32)[:, None, None, None]
    owner_ids = jnp.arange(SPLIT, dtype=jnp.int32)[None, None, :, None]
    row_ids = jnp.arange(slab_rows, dtype=jnp.int32)[None, None, None, :]
    chosen = jnp.transpose(slab_plan, (0, 2, 1))[:, :, :, None].astype(jnp.int32)
    order = (group_ids * (TOK_DEV * SPLIT) + owner_ids * TOK_DEV + chosen * slab_rows + row_ids).reshape(-1).astype(jnp.int32)
    attended = jnp.take(out_nat, order, axis=0)
    query_grads = jnp.take(dq_nat, order, axis=0)
    return (attended, query_grads, key_accumulator[LONGEST_LENGTH:].astype(jnp.bfloat16), value_accumulator[LONGEST_LENGTH:].astype(jnp.bfloat16))
```

```python
import functools
import math

import jax
import jax.numpy as jnp
from jax import lax
from jax.experimental import pallas as pl
from jax.experimental.pallas import tpu as pltpu
from jax.sharding import PartitionSpec as P

KV = 4
W = 128
PER = 8
ROWS = 128
SPLIT = 16
SLAB = ROWS // SPLIT
GROUPS = 8
DOCS = 96
PAIR = 2
MESH = pl.DeviceIdType.MESH
NT = (((1,), (1,)), ((), ()))
SCALE = 1.0 / math.sqrt(W)
LOG2E = math.log2(math.e)


def dot(a, b):
    return jnp.dot(a, b, preferred_element_type=jnp.float32)


def dot_nt(a, b):
    return lax.dot_general(a, b, NT, preferred_element_type=jnp.float32)


def kernel(
    q_hbm, do_hbm, k_hbm, v_hbm, doc_hbm, plan_hbm,
    att_ref, dq_ref, dk_ref, dv_ref,
    q_v, do_v, k_v, v_v, doc_s, plan_s, halo, sendb, recvb, gsend, grecv, own, bias, perm,
    load_sem, small_sem, hsend, hrecv, asend, arecv, aself, gs_sem, gr_sem,
):
    g, c = lax.axis_index("dp"), lax.axis_index("ctx")
    line = g * SPLIT + c
    total = GROUPS * SPLIT

    def along(by):
        other = (line + by + total) % total
        return (other // SPLIT, other % SPLIT)

    barrier = pltpu.get_barrier_semaphore()
    for by in (1, 2, -1, -2):
        pl.semaphore_signal(barrier, inc=1, device_id=along(by), device_id_type=MESH)

    def greet(k, _):
        pl.semaphore_signal(barrier, inc=1, device_id=(g, (c + k) % SPLIT), device_id_type=MESH)
        return 0

    lax.fori_loop(1, SPLIT, greet, 0)

    loads = [
        pltpu.make_async_copy(src, dst, load_sem.at[i])
        for i, (src, dst) in enumerate(((q_hbm, q_v), (do_hbm, do_v), (k_hbm, k_v), (v_hbm, v_v)))
    ]
    smalls = [
        pltpu.make_async_copy(doc_hbm, doc_s, small_sem.at[0]),
        pltpu.make_async_copy(plan_hbm.at[0], plan_s, small_sem.at[1]),
    ]
    for copy in smalls + loads:
        copy.start()

    for copy in smalls:
        copy.wait()
    pos = line * ROWS + lax.broadcasted_iota(jnp.int32, (1, ROWS), 1)

    def add_doc(i, carry):
        end, first = carry
        length = doc_s[i]
        end = end + length
        return end, first + jnp.where(end <= pos, length, 0)

    _, first = lax.fori_loop(0, DOCS, add_doc, (jnp.int32(0), jnp.zeros((1, ROWS), jnp.int32)))
    k_pos = line * ROWS - 2 * ROWS + lax.broadcasted_iota(jnp.int32, (3 * ROWS, ROWS), 0)
    bias[...] = jnp.where((k_pos >= first) & (k_pos <= pos), 0.0, -1e30).astype(jnp.float32)

    r_id = lax.broadcasted_iota(jnp.int32, (2 * SLAB, 2 * ROWS), 0)
    r_id = jnp.where(r_id >= SLAB, r_id - SLAB + ROWS, r_id)
    column = lax.broadcasted_iota(jnp.int32, (2 * SLAB, 2 * ROWS), 1)
    for d in range(SPLIT):
        hit = column == r_id + plan_s[c, d] * SLAB
        perm[d * 2 * SLAB : (d + 1) * 2 * SLAB, :] = jnp.where(hit, 1.0, 0.0).astype(jnp.bfloat16)
    eye = jnp.where(
        lax.broadcasted_iota(jnp.int32, (W, W), 0) == lax.broadcasted_iota(jnp.int32, (W, W), 1),
        1.0,
        0.0,
    ).astype(jnp.bfloat16)

    pl.semaphore_wait(barrier, SPLIT - 1 + 4)

    for h in range(KV):
        for i, src in enumerate((k_hbm, v_hbm)):
            for by in (1, 2):
                pltpu.make_async_remote_copy(
                    src_ref=src.at[:, pl.ds(h * W, W)],
                    dst_ref=halo.at[h, i, pl.ds((2 - by) * ROWS, ROWS)],
                    send_sem=hsend,
                    recv_sem=hrecv.at[h],
                    device_id=along(by),
                    device_id_type=MESH,
                ).start()
    for copy in loads:
        copy.wait()

    def one_head(h, _):
        pltpu.make_async_copy(halo.at[h], halo.at[h], hrecv.at[h]).wait()
        kcol = pl.ds(pl.multiple_of(h * W, W), W)
        kw = jnp.concatenate([halo[h, 0], k_v[:, kcol]], axis=0)
        vw = jnp.concatenate([halo[h, 1], v_v[:, kcol]], axis=0)
        kt = dot_nt(eye, kw).astype(jnp.bfloat16)
        vt = dot_nt(eye, vw).astype(jnp.bfloat16)
        mask = jnp.concatenate([bias[...]] * PAIR, axis=1)
        dk = jnp.zeros((3 * ROWS, W), jnp.float32)
        dv = jnp.zeros((3 * ROWS, W), jnp.float32)
        for p in range(PER // PAIR):
            base = h * (PER * W) + p * PAIR * W
            cols = [pl.ds(pl.multiple_of(base + s * W, W), W) for s in range(PAIR)]
            qs = jnp.concatenate([q_v[:, s] for s in cols], axis=0)
            dos = jnp.concatenate([do_v[:, s] for s in cols], axis=0)
            scores = dot_nt(kw, qs) + mask
            top = jnp.max(scores, axis=0, keepdims=True)
            e = jnp.exp2((scores - top) * (SCALE * LOG2E))
            inv = 1.0 / jnp.sum(e, axis=0, keepdims=True)
            d_probs = dot_nt(vw, dos)
            probs = e * inv
            delta = jnp.sum(probs * d_probs, axis=0, keepdims=True)
            pb = probs.astype(jnp.bfloat16)
            ds = (probs * (d_probs - delta)).astype(jnp.bfloat16)
            dv = dv + dot(pb, dos)
            dk = dk + dot(ds, qs)
            out_t = dot(vt, pb).astype(jnp.bfloat16)
            dq_t = (dot(kt, ds) * SCALE).astype(jnp.bfloat16)
            for s in range(PAIR):
                both = jnp.concatenate(
                    [out_t[:, s * ROWS : (s + 1) * ROWS], dq_t[:, s * ROWS : (s + 1) * ROWS]], axis=1
                )
                message = dot_nt(perm[...], both).astype(jnp.bfloat16)
                sendb[:, :, cols[s]] = message.reshape(SPLIT, 2 * SLAB, W)
            span = pl.ds(pl.multiple_of(base, W), PAIR * W)

            def send(k, _, span=span):
                d = (c + k) % SPLIT
                pltpu.make_async_remote_copy(
                    src_ref=sendb.at[d, :, span],
                    dst_ref=recvb.at[c, :, span],
                    send_sem=asend,
                    recv_sem=arecv.at[h],
                    device_id=(g, d),
                    device_id_type=MESH,
                ).start()
                return 0

            lax.fori_loop(1, SPLIT, send, 0)
        dk = dk * SCALE
        own[h, 0] = dk[2 * ROWS :]
        own[h, 1] = dv[2 * ROWS :]
        gsend[h, 0, 0] = dk[ROWS : 2 * ROWS].astype(jnp.bfloat16)
        gsend[h, 0, 1] = dv[ROWS : 2 * ROWS].astype(jnp.bfloat16)
        gsend[h, 1, 0] = dk[:ROWS].astype(jnp.bfloat16)
        gsend[h, 1, 1] = dv[:ROWS].astype(jnp.bfloat16)
        for by in (1, 2):
            pltpu.make_async_remote_copy(
                src_ref=gsend.at[h, by - 1],
                dst_ref=grecv.at[h, by - 1],
                send_sem=gs_sem,
                recv_sem=gr_sem.at[h],
                device_id=along(-by),
                device_id_type=MESH,
            ).start()
        wide = pl.ds(pl.multiple_of(h * PER * W, W), PER * W)
        pltpu.make_async_copy(sendb.at[c, :, wide], recvb.at[c, :, wide], aself.at[h]).start()
        return 0

    lax.fori_loop(0, KV, one_head, 0)

    def finish(h, _):
        kcol = pl.ds(pl.multiple_of(h * W, W), W)
        wide = pl.ds(pl.multiple_of(h * PER * W, W), PER * W)
        pltpu.make_async_copy(grecv.at[h], grecv.at[h], gr_sem.at[h]).wait()
        for i, ref in enumerate((dk_ref, dv_ref)):
            terms = grecv[h, 0, i].astype(jnp.float32) + grecv[h, 1, i].astype(jnp.float32)
            ref[:, kcol] = (own[h, i] + terms).astype(jnp.bfloat16)
        rest = recvb.at[pl.ds(0, SPLIT - 1), :, wide]
        pltpu.make_async_copy(rest, rest, arecv.at[h]).wait()
        pltpu.make_async_copy(sendb.at[c, :, wide], recvb.at[c, :, wide], aself.at[h]).wait()
        got = recvb[:, :, wide].astype(jnp.float32)
        att_ref[:, wide] = got[:, :SLAB].reshape(ROWS, PER * W).astype(jnp.bfloat16)
        dq_ref[:, wide] = got[:, SLAB:].reshape(ROWS, PER * W).astype(jnp.bfloat16)
        return 0

    lax.fori_loop(0, KV, finish, 0)

    pltpu.make_async_copy(halo, halo, hsend).wait()
    rest = sendb.at[pl.ds(0, SPLIT - 1)]
    pltpu.make_async_copy(rest, rest, asend).wait()
    pltpu.make_async_copy(gsend, gsend, gs_sem).wait()


def on_device(q, k, v, do, doc, plan):
    any_spec = pl.BlockSpec(memory_space=pl.ANY)
    vmem = pl.BlockSpec(memory_space=pltpu.VMEM)
    bf16 = jnp.bfloat16
    return pl.pallas_call(
        kernel,
        out_shape=[
            jax.ShapeDtypeStruct(q.shape, bf16),
            jax.ShapeDtypeStruct(q.shape, bf16),
            jax.ShapeDtypeStruct(k.shape, bf16),
            jax.ShapeDtypeStruct(v.shape, bf16),
        ],
        in_specs=[any_spec] * 6,
        out_specs=[vmem] * 4,
        scratch_shapes=[
            pltpu.VMEM(q.shape, bf16),
            pltpu.VMEM(q.shape, bf16),
            pltpu.VMEM(k.shape, bf16),
            pltpu.VMEM(v.shape, bf16),
            pltpu.SMEM((DOCS,), jnp.int32),
            pltpu.SMEM((SPLIT, SPLIT), jnp.int32),
            pltpu.VMEM((KV, 2, 2 * ROWS, W), bf16),
            pltpu.VMEM((SPLIT, 2 * SLAB, KV * PER * W), bf16),
            pltpu.VMEM((SPLIT, 2 * SLAB, KV * PER * W), bf16),
            pltpu.VMEM((KV, 2, 2, ROWS, W), bf16),
            pltpu.VMEM((KV, 2, 2, ROWS, W), bf16),
            pltpu.VMEM((KV, 2, ROWS, W), jnp.float32),
            pltpu.VMEM((3 * ROWS, ROWS), jnp.float32),
            pltpu.VMEM((2 * ROWS, 2 * ROWS), bf16),
            pltpu.SemaphoreType.DMA((4,)),
            pltpu.SemaphoreType.DMA((2,)),
            pltpu.SemaphoreType.DMA,
            pltpu.SemaphoreType.DMA((KV,)),
            pltpu.SemaphoreType.DMA,
            pltpu.SemaphoreType.DMA((KV,)),
            pltpu.SemaphoreType.DMA((KV,)),
            pltpu.SemaphoreType.DMA,
            pltpu.SemaphoreType.DMA((KV,)),
        ],
        compiler_params=pltpu.CompilerParams(
            collective_id=0, has_side_effects=True, vmem_limit_bytes=60 << 20
        ),
    )(q, do, k, v, doc, plan)


def solution(mesh):
    rows = P(("dp", "ctx"), None)
    return jax.shard_map(
        on_device,
        mesh=mesh,
        in_specs=(rows, rows, rows, rows, P(), P("dp", None, None)),
        out_specs=(rows, rows, rows, rows),
        check_vma=False,
    )
```

```python
import functools
import math

import jax
import jax.numpy as jnp
from jax import lax
from jax.experimental import pallas as pl
from jax.experimental.pallas import tpu as pltpu
from jax.sharding import PartitionSpec as P

KV = 4
W = 128
PER = 8
ROWS = 128
SPLIT = 16
SLAB = ROWS // SPLIT
GROUPS = 8
SIDE = 4
DOCS = 96
PAIR = 2
MESH = pl.DeviceIdType.MESH
NT = (((1,), (1,)), ((), ()))
SCALE = 1.0 / math.sqrt(W)
LOG2E = math.log2(math.e)


def dot(a, b):
    return jnp.dot(a, b, preferred_element_type=jnp.float32)


def dot_nt(a, b):
    return lax.dot_general(a, b, NT, preferred_element_type=jnp.float32)


def kernel(
    q_hbm, do_hbm, k_hbm, v_hbm, doc_hbm, plan_hbm,
    att_ref, dq_ref, dk_ref, dv_ref,
    q_v, do_v, k_v, v_v, doc_s, plan_s, halo, sendb, recvb, gsend, grecv, own, bias, perm,
    load_sem, small_sem, hsend, hrecv, asend, arecv, aself, gs_sem, gr_sem, known,
):
    g, c = lax.axis_index("dp"), lax.axis_index("ctx")
    line = g * SPLIT + c
    total = GROUPS * SPLIT

    def along(by):
        other = (line + by + total) % total
        return (other // SPLIT, other % SPLIT)

    def on_line(by):
        return (line + by >= 0) & (line + by < total)

    y, z = c // SIDE, c % SIDE

    def at(dy, dz):
        return (g, (y + dy) % SIDE * SIDE + (z + dz) % SIDE)

    row = [at(0, by) for by in range(1, SIDE)]
    column = [at(by, 0) for by in range(1, SIDE)]
    barrier = pltpu.get_barrier_semaphore()
    for by in (1, 2, -1, -2):

        @pl.when(on_line(by))
        def _(by=by):
            pl.semaphore_signal(barrier, inc=1, device_id=along(by), device_id_type=MESH)

    for other in row + column:
        pl.semaphore_signal(barrier, inc=1, device_id=other, device_id_type=MESH)

    loads = [
        pltpu.make_async_copy(src, dst, load_sem.at[i])
        for i, (src, dst) in enumerate(((q_hbm, q_v), (do_hbm, do_v), (k_hbm, k_v), (v_hbm, v_v)))
    ]
    smalls = [
        pltpu.make_async_copy(doc_hbm, doc_s, small_sem.at[0]),
        pltpu.make_async_copy(plan_hbm.at[0], plan_s, small_sem.at[1]),
    ]
    for copy in smalls + loads:
        copy.start()

    fill = jnp.zeros((KV, 2, ROWS, W), jnp.bfloat16)
    for by in (1, 2):

        @pl.when(jnp.logical_not(on_line(-by)))
        def _(by=by):
            halo[:, :, (2 - by) * ROWS : (3 - by) * ROWS] = fill

        @pl.when(jnp.logical_not(on_line(by)))
        def _(by=by):
            grecv[:, by - 1] = fill

    near = sum(on_line(by).astype(jnp.int32) for by in (1, 2, -1, -2))
    pl.semaphore_wait(barrier, near + len(row) + len(column))

    for h in range(KV):
        for by in (1, 2):

            @pl.when(on_line(by))
            def _(h=h, by=by):
                for i, src in enumerate((k_hbm, v_hbm)):
                    pltpu.make_async_remote_copy(
                        src_ref=src.at[:, pl.ds(h * W, W)],
                        dst_ref=halo.at[h, i, pl.ds((2 - by) * ROWS, ROWS)],
                        send_sem=hsend.at[by - 1],
                        recv_sem=hrecv.at[h, by - 1],
                        device_id=along(by),
                        device_id_type=MESH,
                    ).start()

    for other in row:
        pl.semaphore_signal(known, inc=1, device_id=other, device_id_type=MESH)

    for copy in smalls:
        copy.wait()
    pos = line * ROWS + lax.broadcasted_iota(jnp.int32, (1, ROWS), 1)

    def add_doc(i, carry):
        end, first = carry
        length = doc_s[i]
        end = end + length
        return end, first + jnp.where(end <= pos, length, 0)

    _, first = lax.fori_loop(0, DOCS, add_doc, (jnp.int32(0), jnp.zeros((1, ROWS), jnp.int32)))
    k_pos = line * ROWS - 2 * ROWS + lax.broadcasted_iota(jnp.int32, (3 * ROWS, ROWS), 0)
    bias[...] = jnp.where((k_pos >= first) & (k_pos <= pos), 0.0, -1e30).astype(jnp.float32)

    r_id = lax.broadcasted_iota(jnp.int32, (2 * SLAB, 2 * ROWS), 0)
    r_id = jnp.where(r_id >= SLAB, r_id - SLAB + ROWS, r_id)
    column = lax.broadcasted_iota(jnp.int32, (2 * SLAB, 2 * ROWS), 1)
    for d in range(SPLIT):
        hit = column == r_id + plan_s[c, d] * SLAB
        perm[d * 2 * SLAB : (d + 1) * 2 * SLAB, :] = jnp.where(hit, 1.0, 0.0).astype(jnp.bfloat16)
    eye = jnp.where(
        lax.broadcasted_iota(jnp.int32, (W, W), 0) == lax.broadcasted_iota(jnp.int32, (W, W), 1),
        1.0,
        0.0,
    ).astype(jnp.bfloat16)

    for copy in loads:
        copy.wait()

    def one_head(h, _):
        for by in (1, 2):

            @pl.when(on_line(-by))
            def _(by=by):
                part = halo.at[h, :, pl.ds((2 - by) * ROWS, ROWS)]
                pltpu.make_async_copy(part, part, hrecv.at[h, by - 1]).wait()

        kcol = pl.ds(pl.multiple_of(h * W, W), W)
        kw = jnp.concatenate([halo[h, 0], k_v[:, kcol]], axis=0)
        vw = jnp.concatenate([halo[h, 1], v_v[:, kcol]], axis=0)
        kt = dot_nt(eye, kw).astype(jnp.bfloat16)
        vt = dot_nt(eye, vw).astype(jnp.bfloat16)
        mask = jnp.concatenate([bias[...]] * PAIR, axis=1)
        dk = jnp.zeros((3 * ROWS, W), jnp.float32)
        dv = jnp.zeros((3 * ROWS, W), jnp.float32)
        for p in range(PER // PAIR):
            base = h * (PER * W) + p * PAIR * W
            cols = [pl.ds(pl.multiple_of(base + s * W, W), W) for s in range(PAIR)]
            qs = jnp.concatenate([q_v[:, s] for s in cols], axis=0)
            dos = jnp.concatenate([do_v[:, s] for s in cols], axis=0)
            scores = dot_nt(kw, qs) + mask
            top = jnp.max(scores, axis=0, keepdims=True)
            e = jnp.exp2((scores - top) * (SCALE * LOG2E))
            inv = 1.0 / jnp.sum(e, axis=0, keepdims=True)
            d_probs = dot_nt(vw, dos)
            probs = e * inv
            delta = jnp.sum(probs * d_probs, axis=0, keepdims=True)
            pb = probs.astype(jnp.bfloat16)
            ds = (probs * (d_probs - delta)).astype(jnp.bfloat16)
            dv = dv + dot(pb, dos)
            dk = dk + dot(ds, qs)
            out_t = dot(vt, pb).astype(jnp.bfloat16)
            dq_t = (dot(kt, ds) * SCALE).astype(jnp.bfloat16)
            for s in range(PAIR):
                both = jnp.concatenate(
                    [out_t[:, s * ROWS : (s + 1) * ROWS], dq_t[:, s * ROWS : (s + 1) * ROWS]], axis=1
                )
                message = dot_nt(perm[...], both).astype(jnp.bfloat16)
                sendb[:, :, cols[s]] = message.reshape(SPLIT, 2 * SLAB, W)
            span = pl.ds(pl.multiple_of(base, W), PAIR * W)

            def send(dy, dz, span=span):
                _, d = at(dy, dz)
                pltpu.make_async_remote_copy(
                    src_ref=sendb.at[d, :, span],
                    dst_ref=recvb.at[c, :, span],
                    send_sem=asend,
                    recv_sem=arecv.at[h],
                    device_id=(g, d),
                    device_id_type=MESH,
                ).start()

            for by in range(1, SIDE):
                send(0, by)
                send(by, 0)
            if p == 0:

                @pl.when(h == 0)
                def _():
                    pl.semaphore_wait(known, SIDE - 1)

            def send_far(k, _, send=send):
                send(k // (SIDE - 1) + 1, (k + k // (SIDE - 1)) % (SIDE - 1) + 1)
                return 0

            lax.fori_loop(0, (SIDE - 1) ** 2, send_far, 0)
        dk = dk * SCALE
        own[h, 0] = dk[2 * ROWS :]
        own[h, 1] = dv[2 * ROWS :]
        gsend[h, 0, 0] = dk[ROWS : 2 * ROWS].astype(jnp.bfloat16)
        gsend[h, 0, 1] = dv[ROWS : 2 * ROWS].astype(jnp.bfloat16)
        gsend[h, 1, 0] = dk[:ROWS].astype(jnp.bfloat16)
        gsend[h, 1, 1] = dv[:ROWS].astype(jnp.bfloat16)
        for by in (1, 2):

            @pl.when(on_line(-by))
            def _(by=by):
                pltpu.make_async_remote_copy(
                    src_ref=gsend.at[h, by - 1],
                    dst_ref=grecv.at[h, by - 1],
                    send_sem=gs_sem.at[by - 1],
                    recv_sem=gr_sem.at[h, by - 1],
                    device_id=along(-by),
                    device_id_type=MESH,
                ).start()

        wide = pl.ds(pl.multiple_of(h * PER * W, W), PER * W)
        pltpu.make_async_copy(sendb.at[c, :, wide], recvb.at[c, :, wide], aself.at[h]).start()
        return 0

    lax.fori_loop(0, KV, one_head, 0)

    def finish(h, _):
        kcol = pl.ds(pl.multiple_of(h * W, W), W)
        wide = pl.ds(pl.multiple_of(h * PER * W, W), PER * W)
        for by in (1, 2):

            @pl.when(on_line(by))
            def _(by=by):
                part = grecv.at[h, by - 1]
                pltpu.make_async_copy(part, part, gr_sem.at[h, by - 1]).wait()

        for i, ref in enumerate((dk_ref, dv_ref)):
            terms = grecv[h, 0, i].astype(jnp.float32) + grecv[h, 1, i].astype(jnp.float32)
            ref[:, kcol] = (own[h, i] + terms).astype(jnp.bfloat16)
        rest = recvb.at[pl.ds(0, SPLIT - 1), :, wide]
        pltpu.make_async_copy(rest, rest, arecv.at[h]).wait()
        pltpu.make_async_copy(sendb.at[c, :, wide], recvb.at[c, :, wide], aself.at[h]).wait()
        got = recvb[:, :, wide].astype(jnp.float32)
        att_ref[:, wide] = got[:, :SLAB].reshape(ROWS, PER * W).astype(jnp.bfloat16)
        dq_ref[:, wide] = got[:, SLAB:].reshape(ROWS, PER * W).astype(jnp.bfloat16)
        return 0

    lax.fori_loop(0, KV, finish, 0)

    for by in (1, 2):

        @pl.when(on_line(by))
        def _(by=by):
            part = halo.at[:, :, pl.ds(0, ROWS)]
            pltpu.make_async_copy(part, part, hsend.at[by - 1]).wait()

        @pl.when(on_line(-by))
        def _(by=by):
            part = gsend.at[:, by - 1]
            pltpu.make_async_copy(part, part, gs_sem.at[by - 1]).wait()

    rest = sendb.at[pl.ds(0, SPLIT - 1)]
    pltpu.make_async_copy(rest, rest, asend).wait()


def write_out(a_in, b_in, c_in, d_in, a_out, b_out, c_out, d_out, sems):
    copies = [
        pltpu.make_async_copy(src, dst, sems.at[i])
        for i, (src, dst) in enumerate(((a_in, a_out), (b_in, b_out), (c_in, c_out), (d_in, d_out)))
    ]
    for copy in copies:
        copy.start()
    for copy in copies:
        copy.wait()


def on_device(q, k, v, do, doc, plan):
    q, k, v, do, doc, plan = (
        pltpu.with_memory_space_constraint(x, pltpu.HBM) for x in (q, k, v, do, doc, plan)
    )
    any_spec = pl.BlockSpec(memory_space=pl.ANY)
    vmem = pl.BlockSpec(memory_space=pltpu.VMEM)
    bf16 = jnp.bfloat16
    parts = pl.pallas_call(
        kernel,
        out_shape=[pltpu.VMEM(x.shape, bf16) for x in (q, q, k, v)],
        in_specs=[any_spec] * 6,
        out_specs=[vmem] * 4,
        scratch_shapes=[
            pltpu.VMEM(q.shape, bf16),
            pltpu.VMEM(q.shape, bf16),
            pltpu.VMEM(k.shape, bf16),
            pltpu.VMEM(v.shape, bf16),
            pltpu.SMEM((DOCS,), jnp.int32),
            pltpu.SMEM((SPLIT, SPLIT), jnp.int32),
            pltpu.VMEM((KV, 2, 2 * ROWS, W), bf16),
            pltpu.VMEM((SPLIT, 2 * SLAB, KV * PER * W), bf16),
            pltpu.VMEM((SPLIT, 2 * SLAB, KV * PER * W), bf16),
            pltpu.VMEM((KV, 2, 2, ROWS, W), bf16),
            pltpu.VMEM((KV, 2, 2, ROWS, W), bf16),
            pltpu.VMEM((KV, 2, ROWS, W), jnp.float32),
            pltpu.VMEM((3 * ROWS, ROWS), jnp.float32),
            pltpu.VMEM((2 * ROWS, 2 * ROWS), bf16),
            pltpu.SemaphoreType.DMA((4,)),
            pltpu.SemaphoreType.DMA((2,)),
            pltpu.SemaphoreType.DMA((2,)),
            pltpu.SemaphoreType.DMA((KV, 2)),
            pltpu.SemaphoreType.DMA,
            pltpu.SemaphoreType.DMA((KV,)),
            pltpu.SemaphoreType.DMA((KV,)),
            pltpu.SemaphoreType.DMA((2,)),
            pltpu.SemaphoreType.DMA((KV, 2)),
            pltpu.SemaphoreType.REGULAR,
        ],
        compiler_params=pltpu.CompilerParams(
            collective_id=0, has_side_effects=True, vmem_limit_bytes=32 << 20
        ),
    )(q, do, k, v, doc, plan)
    return pl.pallas_call(
        write_out,
        out_shape=[jax.ShapeDtypeStruct(x.shape, bf16) for x in (q, q, k, v)],
        in_specs=[any_spec] * 4,
        out_specs=[any_spec] * 4,
        scratch_shapes=[pltpu.SemaphoreType.DMA((4,))],
    )(*(pltpu.with_memory_space_constraint(x, pltpu.VMEM) for x in parts))


def solution(mesh):
    rows = P(("dp", "ctx"), None)
    return jax.shard_map(
        on_device,
        mesh=mesh,
        in_specs=(rows, rows, rows, rows, P(), P("dp", None, None)),
        out_specs=(rows, rows, rows, rows),
        check_vma=False,
    )
```

```python
import functools
import math

import jax
import jax.numpy as jnp
from jax import lax
from jax.experimental import pallas as pl
from jax.experimental.pallas import tpu as pltpu
from jax.sharding import PartitionSpec as P

KV = 4
W = 128
PER = 8
ROWS = 128
SPLIT = 16
SLAB = ROWS // SPLIT
GROUPS = 8
SIDE = 4
DOCS = 96
PAIR = 2
RELAYED = 1
MESH = pl.DeviceIdType.MESH
NT = (((1,), (1,)), ((), ()))
SCALE = 1.0 / math.sqrt(W)
LOG2E = math.log2(math.e)


def dot(a, b):
    return jnp.dot(a, b, preferred_element_type=jnp.float32)


def dot_nt(a, b):
    return lax.dot_general(a, b, NT, preferred_element_type=jnp.float32)


def kernel(
    q_hbm, do_hbm, k_hbm, v_hbm, doc_hbm, plan_hbm,
    att_ref, dq_ref, dk_ref, dv_ref,
    q_v, do_v, k_v, v_v, doc_s, plan_s, halo, sendb, recvb, gsend, grecv, relay, own, bias, perm,
    load_sem, small_sem, hsend, hrecv, asend, arecv, aself, gs_sem, gr_sem, relay_recv, relay_send, known,
):
    g, c = lax.axis_index("dp"), lax.axis_index("ctx")
    line = g * SPLIT + c
    total = GROUPS * SPLIT

    def along(by):
        other = (line + by + total) % total
        return (other // SPLIT, other % SPLIT)

    odd = line % 2 == 1
    even = line % 2 == 0

    def on_line(by):
        return (line + by >= 0) & (line + by < total)

    y, z = c // SIDE, c % SIDE

    def at(dy, dz):
        return (g, (y + dy) % SIDE * SIDE + (z + dz) % SIDE)

    row = [at(0, by) for by in range(1, SIDE)]
    column = [at(by, 0) for by in range(1, SIDE)]
    barrier = pltpu.get_barrier_semaphore()
    for by in (1, 2, -1, -2):

        @pl.when(on_line(by))
        def _(by=by):
            pl.semaphore_signal(barrier, inc=1, device_id=along(by), device_id_type=MESH)

    for other in row + column:
        pl.semaphore_signal(barrier, inc=1, device_id=other, device_id_type=MESH)

    loads = [
        pltpu.make_async_copy(src, dst, load_sem.at[i])
        for i, (src, dst) in enumerate(((q_hbm, q_v), (do_hbm, do_v), (k_hbm, k_v), (v_hbm, v_v)))
    ]
    smalls = [
        pltpu.make_async_copy(doc_hbm, doc_s, small_sem.at[0]),
        pltpu.make_async_copy(plan_hbm.at[0], plan_s, small_sem.at[1]),
    ]
    for copy in smalls + loads:
        copy.start()

    fill = jnp.zeros((KV, 2, ROWS, W), jnp.bfloat16)
    for by in (1, 2):

        @pl.when(jnp.logical_not(on_line(-by)))
        def _(by=by):
            halo[:, :, (2 - by) * ROWS : (3 - by) * ROWS] = fill

        @pl.when(jnp.logical_not(on_line(by)))
        def _(by=by):
            grecv[:, by - 1] = fill

    near = sum(on_line(by).astype(jnp.int32) for by in (1, 2, -1, -2))
    pl.semaphore_wait(barrier, near + len(row) + len(column))

    for h in range(KV):
        for by in (2, 1):

            @pl.when(on_line(by))
            def _(h=h, by=by):
                for i, src in enumerate((k_hbm, v_hbm)):
                    pltpu.make_async_remote_copy(
                        src_ref=src.at[:, pl.ds(h * W, W)],
                        dst_ref=halo.at[h, i, pl.ds((2 - by) * ROWS, ROWS)],
                        send_sem=hsend.at[by - 1],
                        recv_sem=hrecv.at[h, by - 1],
                        device_id=along(by),
                        device_id_type=MESH,
                    ).start()

    for other in row:
        pl.semaphore_signal(known, inc=1, device_id=other, device_id_type=MESH)

    for copy in smalls:
        copy.wait()
    pos = line * ROWS + lax.broadcasted_iota(jnp.int32, (1, ROWS), 1)

    def add_doc(i, carry):
        end, first = carry
        length = doc_s[i]
        end = end + length
        return end, first + jnp.where(end <= pos, length, 0)

    _, first = lax.fori_loop(0, DOCS, add_doc, (jnp.int32(0), jnp.zeros((1, ROWS), jnp.int32)))
    k_pos = line * ROWS - 2 * ROWS + lax.broadcasted_iota(jnp.int32, (3 * ROWS, ROWS), 0)
    bias[...] = jnp.where((k_pos >= first) & (k_pos <= pos), 0.0, -1e30).astype(jnp.float32)

    r_id = lax.broadcasted_iota(jnp.int32, (2 * SLAB, 2 * ROWS), 0)
    r_id = jnp.where(r_id >= SLAB, r_id - SLAB + ROWS, r_id)
    column = lax.broadcasted_iota(jnp.int32, (2 * SLAB, 2 * ROWS), 1)
    for d in range(SPLIT):
        hit = column == r_id + plan_s[c, d] * SLAB
        perm[d * 2 * SLAB : (d + 1) * 2 * SLAB, :] = jnp.where(hit, 1.0, 0.0).astype(jnp.bfloat16)
    eye = jnp.where(
        lax.broadcasted_iota(jnp.int32, (W, W), 0) == lax.broadcasted_iota(jnp.int32, (W, W), 1),
        1.0,
        0.0,
    ).astype(jnp.bfloat16)

    for copy in loads:
        copy.wait()

    def one_head(h, _):
        for by in (1, 2):

            @pl.when(on_line(-by))
            def _(by=by):
                part = halo.at[h, :, pl.ds((2 - by) * ROWS, ROWS)]
                pltpu.make_async_copy(part, part, hrecv.at[h, by - 1]).wait()

        kcol = pl.ds(pl.multiple_of(h * W, W), W)
        kw = jnp.concatenate([halo[h, 0], k_v[:, kcol]], axis=0)
        vw = jnp.concatenate([halo[h, 1], v_v[:, kcol]], axis=0)
        kt = dot_nt(eye, kw).astype(jnp.bfloat16)
        vt = dot_nt(eye, vw).astype(jnp.bfloat16)
        mask = jnp.concatenate([bias[...]] * PAIR, axis=1)
        dk = jnp.zeros((3 * ROWS, W), jnp.float32)
        dv = jnp.zeros((3 * ROWS, W), jnp.float32)
        for p in range(PER // PAIR):
            base = h * (PER * W) + p * PAIR * W
            cols = [pl.ds(pl.multiple_of(base + s * W, W), W) for s in range(PAIR)]
            qs = jnp.concatenate([q_v[:, s] for s in cols], axis=0)
            dos = jnp.concatenate([do_v[:, s] for s in cols], axis=0)
            scores = dot_nt(kw, qs) + mask
            top = jnp.max(scores, axis=0, keepdims=True)
            e = jnp.exp2((scores - top) * (SCALE * LOG2E))
            inv = 1.0 / jnp.sum(e, axis=0, keepdims=True)
            d_probs = dot_nt(vw, dos)
            probs = e * inv
            delta = jnp.sum(probs * d_probs, axis=0, keepdims=True)
            pb = probs.astype(jnp.bfloat16)
            ds = (probs * (d_probs - delta)).astype(jnp.bfloat16)
            dv = dv + dot(pb, dos)
            dk = dk + dot(ds, qs)
            out_t = dot(vt, pb).astype(jnp.bfloat16)
            dq_t = (dot(kt, ds) * SCALE).astype(jnp.bfloat16)
            for s in range(PAIR):
                both = jnp.concatenate(
                    [out_t[:, s * ROWS : (s + 1) * ROWS], dq_t[:, s * ROWS : (s + 1) * ROWS]], axis=1
                )
                message = dot_nt(perm[...], both).astype(jnp.bfloat16)
                sendb[:, :, cols[s]] = message.reshape(SPLIT, 2 * SLAB, W)
            span = pl.ds(pl.multiple_of(base, W), PAIR * W)

            def send(dy, dz, span=span):
                _, d = at(dy, dz)
                pltpu.make_async_remote_copy(
                    src_ref=sendb.at[d, :, span],
                    dst_ref=recvb.at[c, :, span],
                    send_sem=asend,
                    recv_sem=arecv.at[h],
                    device_id=(g, d),
                    device_id_type=MESH,
                ).start()

            for by in range(1, SIDE):
                send(0, by)
                send(by, 0)
            if p == 0:

                @pl.when(h == 0)
                def _():
                    pl.semaphore_wait(known, SIDE - 1)

            def send_far(k, _, send=send):
                send(k // (SIDE - 1) + 1, (k + k // (SIDE - 1)) % (SIDE - 1) + 1)
                return 0

            lax.fori_loop(0, (SIDE - 1) ** 2, send_far, 0)
        dk = dk * SCALE
        own[h, 0] = dk[2 * ROWS :]
        own[h, 1] = dv[2 * ROWS :]
        gsend[h, 0, 0] = dk[ROWS : 2 * ROWS].astype(jnp.bfloat16)
        gsend[h, 0, 1] = dv[ROWS : 2 * ROWS].astype(jnp.bfloat16)
        gsend[h, 1, 0] = dk[:ROWS].astype(jnp.bfloat16)
        gsend[h, 1, 1] = dv[:ROWS].astype(jnp.bfloat16)
        def give(by, dst, sem, other):
            pltpu.make_async_remote_copy(
                src_ref=gsend.at[h, by - 1],
                dst_ref=dst,
                send_sem=gs_sem.at[by - 1],
                recv_sem=sem,
                device_id=other,
                device_id_type=MESH,
            ).start()

        @pl.when(on_line(-1))
        def _():
            give(1, grecv.at[h, 0], gr_sem.at[h, 0], along(-1))

        around = odd & (h < RELAYED) & ((z != 1) | (y != 0))

        @pl.when(on_line(-2) & jnp.logical_not(around))
        def _():
            give(2, grecv.at[h, 1], gr_sem.at[h, 1], along(-2))

        @pl.when(on_line(-2) & around)
        def _():
            give(2, relay.at[h], relay_recv.at[h], at(0, 1))

        wide = pl.ds(pl.multiple_of(h * PER * W, W), PER * W)
        pltpu.make_async_copy(sendb.at[c, :, wide], recvb.at[c, :, wide], aself.at[h]).start()
        return 0

    lax.fori_loop(0, KV, one_head, 0)

    below = line - z + (z + SIDE - 1) % SIDE
    carries = even & (below >= 2) & ((z != 2) | (y != 0))

    @pl.when(carries)
    def _():
        for h in range(RELAYED):
            pltpu.make_async_copy(relay.at[h], relay.at[h], relay_recv.at[h]).wait()
            pltpu.make_async_remote_copy(
                src_ref=relay.at[h],
                dst_ref=grecv.at[h, 1],
                send_sem=relay_send,
                recv_sem=gr_sem.at[h, 1],
                device_id=((below - 2) // SPLIT, (below - 2) % SPLIT),
                device_id_type=MESH,
            ).start()


    def finish(h, _):
        kcol = pl.ds(pl.multiple_of(h * W, W), W)
        wide = pl.ds(pl.multiple_of(h * PER * W, W), PER * W)
        for by in (1, 2):

            @pl.when(on_line(by))
            def _(by=by):
                part = grecv.at[h, by - 1]
                pltpu.make_async_copy(part, part, gr_sem.at[h, by - 1]).wait()

        for i, ref in enumerate((dk_ref, dv_ref)):
            terms = grecv[h, 0, i].astype(jnp.float32) + grecv[h, 1, i].astype(jnp.float32)
            ref[:, kcol] = (own[h, i] + terms).astype(jnp.bfloat16)
        rest = recvb.at[pl.ds(0, SPLIT - 1), :, wide]
        pltpu.make_async_copy(rest, rest, arecv.at[h]).wait()
        pltpu.make_async_copy(sendb.at[c, :, wide], recvb.at[c, :, wide], aself.at[h]).wait()
        got = recvb[:, :, wide].astype(jnp.float32)
        att_ref[:, wide] = got[:, :SLAB].reshape(ROWS, PER * W).astype(jnp.bfloat16)
        dq_ref[:, wide] = got[:, SLAB:].reshape(ROWS, PER * W).astype(jnp.bfloat16)
        return 0

    lax.fori_loop(0, KV, finish, 0)

    for by in (1, 2):

        @pl.when(on_line(by))
        def _(by=by):
            part = halo.at[:, :, pl.ds(0, ROWS)]
            pltpu.make_async_copy(part, part, hsend.at[by - 1]).wait()

        @pl.when(on_line(-by))
        def _(by=by):
            part = gsend.at[:, by - 1]
            pltpu.make_async_copy(part, part, gs_sem.at[by - 1]).wait()

    rest = sendb.at[pl.ds(0, SPLIT - 1)]
    pltpu.make_async_copy(rest, rest, asend).wait()

    @pl.when(carries)
    def _():
        pltpu.make_async_copy(relay, relay, relay_send).wait()


def write_out(a_in, b_in, c_in, d_in, a_out, b_out, c_out, d_out, sems):
    copies = [
        pltpu.make_async_copy(src, dst, sems.at[i])
        for i, (src, dst) in enumerate(((a_in, a_out), (b_in, b_out), (c_in, c_out), (d_in, d_out)))
    ]
    for copy in copies:
        copy.start()
    for copy in copies:
        copy.wait()


def on_device(q, k, v, do, doc, plan):
    q, k, v, do, doc, plan = (
        pltpu.with_memory_space_constraint(x, pltpu.HBM) for x in (q, k, v, do, doc, plan)
    )
    any_spec = pl.BlockSpec(memory_space=pl.ANY)
    vmem = pl.BlockSpec(memory_space=pltpu.VMEM)
    bf16 = jnp.bfloat16
    parts = pl.pallas_call(
        kernel,
        out_shape=[pltpu.VMEM(x.shape, bf16) for x in (q, q, k, v)],
        in_specs=[any_spec] * 6,
        out_specs=[vmem] * 4,
        scratch_shapes=[
            pltpu.VMEM(q.shape, bf16),
            pltpu.VMEM(q.shape, bf16),
            pltpu.VMEM(k.shape, bf16),
            pltpu.VMEM(v.shape, bf16),
            pltpu.SMEM((DOCS,), jnp.int32),
            pltpu.SMEM((SPLIT, SPLIT), jnp.int32),
            pltpu.VMEM((KV, 2, 2 * ROWS, W), bf16),
            pltpu.VMEM((SPLIT, 2 * SLAB, KV * PER * W), bf16),
            pltpu.VMEM((SPLIT, 2 * SLAB, KV * PER * W), bf16),
            pltpu.VMEM((KV, 2, 2, ROWS, W), bf16),
            pltpu.VMEM((KV, 2, 2, ROWS, W), bf16),
            pltpu.VMEM((RELAYED, 2, ROWS, W), bf16),
            pltpu.VMEM((KV, 2, ROWS, W), jnp.float32),
            pltpu.VMEM((3 * ROWS, ROWS), jnp.float32),
            pltpu.VMEM((2 * ROWS, 2 * ROWS), bf16),
            pltpu.SemaphoreType.DMA((4,)),
            pltpu.SemaphoreType.DMA((2,)),
            pltpu.SemaphoreType.DMA((2,)),
            pltpu.SemaphoreType.DMA((KV, 2)),
            pltpu.SemaphoreType.DMA,
            pltpu.SemaphoreType.DMA((KV,)),
            pltpu.SemaphoreType.DMA((KV,)),
            pltpu.SemaphoreType.DMA((2,)),
            pltpu.SemaphoreType.DMA((KV, 2)),
            pltpu.SemaphoreType.DMA((RELAYED,)),
            pltpu.SemaphoreType.DMA,
            pltpu.SemaphoreType.REGULAR,
        ],
        compiler_params=pltpu.CompilerParams(
            collective_id=0, has_side_effects=True, vmem_limit_bytes=32 << 20
        ),
    )(q, do, k, v, doc, plan)
    return pl.pallas_call(
        write_out,
        out_shape=[jax.ShapeDtypeStruct(x.shape, bf16) for x in (q, q, k, v)],
        in_specs=[any_spec] * 4,
        out_specs=[any_spec] * 4,
        scratch_shapes=[pltpu.SemaphoreType.DMA((4,))],
    )(*(pltpu.with_memory_space_constraint(x, pltpu.VMEM) for x in parts))


def solution(mesh):
    rows = P(("dp", "ctx"), None)
    return jax.shard_map(
        on_device,
        mesh=mesh,
        in_specs=(rows, rows, rows, rows, P(), P("dp", None, None)),
        out_specs=(rows, rows, rows, rows),
        check_vma=False,
    )
```

```python
import functools
import math

import jax
import jax.numpy as jnp
from jax import lax
from jax.experimental import pallas as pl
from jax.experimental.pallas import tpu as pltpu
from jax.sharding import PartitionSpec as P

KV = 4
W = 128
PER = 8
ROWS = 128
SPLIT = 16
SLAB = ROWS // SPLIT
GROUPS = 8
SIDE = 4
DOCS = 96
PAIR = 2
RELAYED = 1
MESH = pl.DeviceIdType.MESH
NT = (((1,), (1,)), ((), ()))
SCALE = 1.0 / math.sqrt(W)
LOG2E = math.log2(math.e)


def dot(a, b):
    return jnp.dot(a, b, preferred_element_type=jnp.float32)


def dot_nt(a, b):
    return lax.dot_general(a, b, NT, preferred_element_type=jnp.float32)


def kernel(
    q_hbm, do_hbm, k_hbm, v_hbm, doc_hbm, plan_hbm,
    att_ref, dq_ref, dk_ref, dv_ref,
    q_v, do_v, k_v, v_v, doc_s, plan_s, halo, sendb, recvb, gsend, grecv, relay, own, bias, perm,
    load_sem, small_sem, hsend, hrecv, asend, arecv, aself, gs_sem, gr_sem, relay_recv, relay_send, known,
):
    g, c = lax.axis_index("dp"), lax.axis_index("ctx")
    line = g * SPLIT + c
    total = GROUPS * SPLIT

    def along(by):
        other = (line + by + total) % total
        return (other // SPLIT, other % SPLIT)

    odd = line % 2 == 1
    even = line % 2 == 0

    def on_line(by):
        return (line + by >= 0) & (line + by < total)

    y, z = c // SIDE, c % SIDE

    def at(dy, dz):
        return (g, (y + dy) % SIDE * SIDE + (z + dz) % SIDE)

    row = [at(0, by) for by in range(1, SIDE)]
    column = [at(by, 0) for by in range(1, SIDE)]
    barrier = pltpu.get_barrier_semaphore()
    for by in (1, 2, -1, -2):

        @pl.when(on_line(by))
        def _(by=by):
            pl.semaphore_signal(barrier, inc=1, device_id=along(by), device_id_type=MESH)

    for other in row + column:
        pl.semaphore_signal(barrier, inc=1, device_id=other, device_id_type=MESH)

    loads = [
        pltpu.make_async_copy(src, dst, load_sem.at[i])
        for i, (src, dst) in enumerate(((q_hbm, q_v), (do_hbm, do_v), (k_hbm, k_v), (v_hbm, v_v)))
    ]
    smalls = [
        pltpu.make_async_copy(doc_hbm, doc_s, small_sem.at[0]),
        pltpu.make_async_copy(plan_hbm.at[0], plan_s, small_sem.at[1]),
    ]
    for copy in smalls + loads:
        copy.start()

    fill = jnp.zeros((KV, 2, ROWS, W), jnp.bfloat16)
    for by in (1, 2):

        @pl.when(jnp.logical_not(on_line(-by)))
        def _(by=by):
            halo[:, :, (2 - by) * ROWS : (3 - by) * ROWS] = fill

        @pl.when(jnp.logical_not(on_line(by)))
        def _(by=by):
            grecv[:, by - 1] = fill

    near = sum(on_line(by).astype(jnp.int32) for by in (1, 2, -1, -2))
    pl.semaphore_wait(barrier, near + len(row) + len(column))

    far_first = [(0, 2), (0, 1)] + [(h, by) for by in (2, 1) for h in range(1, KV)]
    for h, by in far_first:
        if True:

            @pl.when(on_line(by))
            def _(h=h, by=by):
                for i, src in enumerate((k_hbm, v_hbm)):
                    pltpu.make_async_remote_copy(
                        src_ref=src.at[:, pl.ds(h * W, W)],
                        dst_ref=halo.at[h, i, pl.ds((2 - by) * ROWS, ROWS)],
                        send_sem=hsend.at[by - 1],
                        recv_sem=hrecv.at[h, by - 1],
                        device_id=along(by),
                        device_id_type=MESH,
                    ).start()

    for other in row:
        pl.semaphore_signal(known, inc=1, device_id=other, device_id_type=MESH)

    for copy in smalls:
        copy.wait()
    pos = line * ROWS + lax.broadcasted_iota(jnp.int32, (1, ROWS), 1)

    def add_doc(i, carry):
        end, first = carry
        length = doc_s[i]
        end = end + length
        return end, first + jnp.where(end <= pos, length, 0)

    _, first = lax.fori_loop(0, DOCS, add_doc, (jnp.int32(0), jnp.zeros((1, ROWS), jnp.int32)))
    k_pos = line * ROWS - 2 * ROWS + lax.broadcasted_iota(jnp.int32, (3 * ROWS, ROWS), 0)
    bias[...] = jnp.where((k_pos >= first) & (k_pos <= pos), 0.0, -1e30).astype(jnp.float32)

    r_id = lax.broadcasted_iota(jnp.int32, (2 * SLAB, 2 * ROWS), 0)
    r_id = jnp.where(r_id >= SLAB, r_id - SLAB + ROWS, r_id)
    column = lax.broadcasted_iota(jnp.int32, (2 * SLAB, 2 * ROWS), 1)
    for d in range(SPLIT):
        hit = column == r_id + plan_s[c, d] * SLAB
        perm[d * 2 * SLAB : (d + 1) * 2 * SLAB, :] = jnp.where(hit, 1.0, 0.0).astype(jnp.bfloat16)
    eye = jnp.where(
        lax.broadcasted_iota(jnp.int32, (W, W), 0) == lax.broadcasted_iota(jnp.int32, (W, W), 1),
        1.0,
        0.0,
    ).astype(jnp.bfloat16)

    for copy in loads:
        copy.wait()

    def one_head(h, _):
        for by in (1, 2):

            @pl.when(on_line(-by))
            def _(by=by):
                part = halo.at[h, :, pl.ds((2 - by) * ROWS, ROWS)]
                pltpu.make_async_copy(part, part, hrecv.at[h, by - 1]).wait()

        kcol = pl.ds(pl.multiple_of(h * W, W), W)
        kw = jnp.concatenate([halo[h, 0], k_v[:, kcol]], axis=0)
        vw = jnp.concatenate([halo[h, 1], v_v[:, kcol]], axis=0)
        kt = dot_nt(eye, kw).astype(jnp.bfloat16)
        vt = dot_nt(eye, vw).astype(jnp.bfloat16)
        mask = jnp.concatenate([bias[...]] * PAIR, axis=1)
        dk = jnp.zeros((3 * ROWS, W), jnp.float32)
        dv = jnp.zeros((3 * ROWS, W), jnp.float32)
        for p in range(PER // PAIR):
            base = h * (PER * W) + p * PAIR * W
            cols = [pl.ds(pl.multiple_of(base + s * W, W), W) for s in range(PAIR)]
            qs = jnp.concatenate([q_v[:, s] for s in cols], axis=0)
            dos = jnp.concatenate([do_v[:, s] for s in cols], axis=0)
            scores = dot_nt(kw, qs) + mask
            top = jnp.max(scores, axis=0, keepdims=True)
            e = jnp.exp2((scores - top) * (SCALE * LOG2E))
            inv = 1.0 / jnp.sum(e, axis=0, keepdims=True)
            d_probs = dot_nt(vw, dos)
            probs = e * inv
            delta = jnp.sum(probs * d_probs, axis=0, keepdims=True)
            pb = probs.astype(jnp.bfloat16)
            ds = (probs * (d_probs - delta)).astype(jnp.bfloat16)
            dv = dv + dot(pb, dos)
            dk = dk + dot(ds, qs)
            out_t = dot(vt, pb).astype(jnp.bfloat16)
            dq_t = (dot(kt, ds) * SCALE).astype(jnp.bfloat16)
            for s in range(PAIR):
                both = jnp.concatenate(
                    [out_t[:, s * ROWS : (s + 1) * ROWS], dq_t[:, s * ROWS : (s + 1) * ROWS]], axis=1
                )
                message = dot_nt(perm[...], both).astype(jnp.bfloat16)
                sendb[:, :, cols[s]] = message.reshape(SPLIT, 2 * SLAB, W)
            span = pl.ds(pl.multiple_of(base, W), PAIR * W)

            def send(dy, dz, span=span):
                _, d = at(dy, dz)
                pltpu.make_async_remote_copy(
                    src_ref=sendb.at[d, :, span],
                    dst_ref=recvb.at[c, :, span],
                    send_sem=asend,
                    recv_sem=arecv.at[h],
                    device_id=(g, d),
                    device_id_type=MESH,
                ).start()

            @pl.when(h == KV - 1)
            def _(send=send):
                for far in range(2 * SIDE - 1):
                    for ty in range(SIDE):
                        if 0 <= far - ty < SIDE:

                            @pl.when(c != ty * SIDE + far - ty)
                            def _(ty=ty, tz=far - ty):
                                send(ty - y + SIDE, tz - z + SIDE)

            @pl.when(h < KV - 1)
            def _(send=send):
                for by in range(1, SIDE):
                    send(0, by)
                    send(by, 0)

            if p == 0:

                @pl.when(h == 0)
                def _():
                    pl.semaphore_wait(known, SIDE - 1)

            def send_far(k, _, send=send):
                send(k // (SIDE - 1) + 1, (k + k // (SIDE - 1)) % (SIDE - 1) + 1)
                return 0

            @pl.when(h < KV - 1)
            def _(send_far=send_far):
                lax.fori_loop(0, (SIDE - 1) ** 2, send_far, 0)

        dk = dk * SCALE
        own[h, 0] = dk[2 * ROWS :]
        own[h, 1] = dv[2 * ROWS :]
        gsend[h, 0, 0] = dk[ROWS : 2 * ROWS].astype(jnp.bfloat16)
        gsend[h, 0, 1] = dv[ROWS : 2 * ROWS].astype(jnp.bfloat16)
        gsend[h, 1, 0] = dk[:ROWS].astype(jnp.bfloat16)
        gsend[h, 1, 1] = dv[:ROWS].astype(jnp.bfloat16)
        def give(by, dst, sem, other):
            pltpu.make_async_remote_copy(
                src_ref=gsend.at[h, by - 1],
                dst_ref=dst,
                send_sem=gs_sem.at[by - 1],
                recv_sem=sem,
                device_id=other,
                device_id_type=MESH,
            ).start()

        @pl.when(on_line(-1))
        def _():
            give(1, grecv.at[h, 0], gr_sem.at[h, 0], along(-1))

        around = odd & (h < RELAYED) & ((z != 1) | (y != 0))

        @pl.when(on_line(-2) & jnp.logical_not(around))
        def _():
            give(2, grecv.at[h, 1], gr_sem.at[h, 1], along(-2))

        @pl.when(on_line(-2) & around)
        def _():
            give(2, relay.at[h], relay_recv.at[h], at(0, 1))

        wide = pl.ds(pl.multiple_of(h * PER * W, W), PER * W)
        pltpu.make_async_copy(sendb.at[c, :, wide], recvb.at[c, :, wide], aself.at[h]).start()
        return 0

    lax.fori_loop(0, KV, one_head, 0)

    below = line - z + (z + SIDE - 1) % SIDE
    carries = even & (below >= 2) & ((z != 2) | (y != 0))

    @pl.when(carries)
    def _():
        for h in range(RELAYED):
            pltpu.make_async_copy(relay.at[h], relay.at[h], relay_recv.at[h]).wait()
            pltpu.make_async_remote_copy(
                src_ref=relay.at[h],
                dst_ref=grecv.at[h, 1],
                send_sem=relay_send,
                recv_sem=gr_sem.at[h, 1],
                device_id=((below - 2) // SPLIT, (below - 2) % SPLIT),
                device_id_type=MESH,
            ).start()


    def finish(h, _):
        kcol = pl.ds(pl.multiple_of(h * W, W), W)
        wide = pl.ds(pl.multiple_of(h * PER * W, W), PER * W)
        for by in (1, 2):

            @pl.when(on_line(by))
            def _(by=by):
                part = grecv.at[h, by - 1]
                pltpu.make_async_copy(part, part, gr_sem.at[h, by - 1]).wait()

        for i, ref in enumerate((dk_ref, dv_ref)):
            terms = grecv[h, 0, i].astype(jnp.float32) + grecv[h, 1, i].astype(jnp.float32)
            ref[:, kcol] = (own[h, i] + terms).astype(jnp.bfloat16)
        rest = recvb.at[pl.ds(0, SPLIT - 1), :, wide]
        pltpu.make_async_copy(rest, rest, arecv.at[h]).wait()
        pltpu.make_async_copy(sendb.at[c, :, wide], recvb.at[c, :, wide], aself.at[h]).wait()
        got = recvb[:, :, wide].astype(jnp.float32)
        att_ref[:, wide] = got[:, :SLAB].reshape(ROWS, PER * W).astype(jnp.bfloat16)
        dq_ref[:, wide] = got[:, SLAB:].reshape(ROWS, PER * W).astype(jnp.bfloat16)
        return 0

    lax.fori_loop(0, KV, finish, 0)

    for by in (1, 2):

        @pl.when(on_line(by))
        def _(by=by):
            part = halo.at[:, :, pl.ds(0, ROWS)]
            pltpu.make_async_copy(part, part, hsend.at[by - 1]).wait()

        @pl.when(on_line(-by))
        def _(by=by):
            part = gsend.at[:, by - 1]
            pltpu.make_async_copy(part, part, gs_sem.at[by - 1]).wait()

    rest = sendb.at[pl.ds(0, SPLIT - 1)]
    pltpu.make_async_copy(rest, rest, asend).wait()

    @pl.when(carries)
    def _():
        pltpu.make_async_copy(relay, relay, relay_send).wait()


def write_out(a_in, b_in, c_in, d_in, a_out, b_out, c_out, d_out, sems):
    copies = [
        pltpu.make_async_copy(src, dst, sems.at[i])
        for i, (src, dst) in enumerate(((a_in, a_out), (b_in, b_out), (c_in, c_out), (d_in, d_out)))
    ]
    for copy in copies:
        copy.start()
    for copy in copies:
        copy.wait()


def on_device(q, k, v, do, doc, plan):
    q, k, v, do, doc, plan = (
        pltpu.with_memory_space_constraint(x, pltpu.HBM) for x in (q, k, v, do, doc, plan)
    )
    any_spec = pl.BlockSpec(memory_space=pl.ANY)
    vmem = pl.BlockSpec(memory_space=pltpu.VMEM)
    bf16 = jnp.bfloat16
    parts = pl.pallas_call(
        kernel,
        out_shape=[pltpu.VMEM(x.shape, bf16) for x in (q, q, k, v)],
        in_specs=[any_spec] * 6,
        out_specs=[vmem] * 4,
        scratch_shapes=[
            pltpu.VMEM(q.shape, bf16),
            pltpu.VMEM(q.shape, bf16),
            pltpu.VMEM(k.shape, bf16),
            pltpu.VMEM(v.shape, bf16),
            pltpu.SMEM((DOCS,), jnp.int32),
            pltpu.SMEM((SPLIT, SPLIT), jnp.int32),
            pltpu.VMEM((KV, 2, 2 * ROWS, W), bf16),
            pltpu.VMEM((SPLIT, 2 * SLAB, KV * PER * W), bf16),
            pltpu.VMEM((SPLIT, 2 * SLAB, KV * PER * W), bf16),
            pltpu.VMEM((KV, 2, 2, ROWS, W), bf16),
            pltpu.VMEM((KV, 2, 2, ROWS, W), bf16),
            pltpu.VMEM((RELAYED, 2, ROWS, W), bf16),
            pltpu.VMEM((KV, 2, ROWS, W), jnp.float32),
            pltpu.VMEM((3 * ROWS, ROWS), jnp.float32),
            pltpu.VMEM((2 * ROWS, 2 * ROWS), bf16),
            pltpu.SemaphoreType.DMA((4,)),
            pltpu.SemaphoreType.DMA((2,)),
            pltpu.SemaphoreType.DMA((2,)),
            pltpu.SemaphoreType.DMA((KV, 2)),
            pltpu.SemaphoreType.DMA,
            pltpu.SemaphoreType.DMA((KV,)),
            pltpu.SemaphoreType.DMA((KV,)),
            pltpu.SemaphoreType.DMA((2,)),
            pltpu.SemaphoreType.DMA((KV, 2)),
            pltpu.SemaphoreType.DMA((RELAYED,)),
            pltpu.SemaphoreType.DMA,
            pltpu.SemaphoreType.REGULAR,
        ],
        compiler_params=pltpu.CompilerParams(
            collective_id=0, has_side_effects=True, vmem_limit_bytes=32 << 20
        ),
    )(q, do, k, v, doc, plan)
    return pl.pallas_call(
        write_out,
        out_shape=[jax.ShapeDtypeStruct(x.shape, bf16) for x in (q, q, k, v)],
        in_specs=[any_spec] * 4,
        out_specs=[any_spec] * 4,
        scratch_shapes=[pltpu.SemaphoreType.DMA((4,))],
    )(*(pltpu.with_memory_space_constraint(x, pltpu.VMEM) for x in parts))


def solution(mesh):
    rows = P(("dp", "ctx"), None)
    return jax.shard_map(
        on_device,
        mesh=mesh,
        in_specs=(rows, rows, rows, rows, P(), P("dp", None, None)),
        out_specs=(rows, rows, rows, rows),
        check_vma=False,
    )
```
